512 devices in a mesh: kv: 64 (over z, x), head: 8 (over y, core).
Axes of the slice: x: 4, y: 4, z: 16, core: 2. Of those that a mesh axis runs over, the one named last changes fastest.
Arguments:
- query: bfloat16 [8, 64, 128], P(None, 'head'), may hold values from -144 to 144
- key_cache: bfloat16 [8, 8, 24576, 128], P(None, 'head', 'kv'), may hold values from -6 to 6
- value_cache: bfloat16 [8, 8, 24576, 128], P(None, 'head', 'kv'), may hold values from -6 to 6
- lengths: int32 [8], replicated, may hold values from 2 to 24576, as said below
- residual: bfloat16 [8, 8192], P(None, 'kv'), may hold values from -41 to 41
- out_weight: bfloat16 [8192, 8192], P('head', 'kv'), may hold values from -0.0625 to 0.0625
- norm_gain: bfloat16 [8192], P('kv'), may hold values from 0.25 to 1.75
- gate_weight: bfloat16 [8192, 28672], P('kv', 'head'), may hold values from -0.1875 to 0.1875
- up_weight: bfloat16 [8192, 28672], P('kv', 'head'), may hold values from -0.1875 to 0.1875
- down_weight: bfloat16 [28672, 8192], P('head', 'kv'), may hold values from -0.03125 to 0.03125
Outputs:
- mixed: bfloat16 [8, 8192], P(None, 'kv')
The draws below stay inside these ranges and needn't reach their ends.
Inputs may be any that keep to these rules, and one draw needn't show every extreme that they name: `lengths`: each sequence has 2 to 24576 live slots, the first ones; some sequence has exactly 24576.
All inputs are finite; a program needn't handle non-finite values.
Results may differ from the reference program's by a relative error of at most 0.023.
Values may be sent and summed in bfloat16 or wider, within the bound.
No kernel may reach another device: no remote copies, remote signals or barrier semaphores. Data moves between devices by JAX's collectives and lax.ppermute only.
A program may use at most 64 MiB of HBM per device.

```python
import math
import jax
import jax.numpy as jnp
from jax import lax

D = 8192
HEADS = 64
KVH = 8
HD = 128
FF = 28672
SEQS = 8
CACHE = 24576


def shared_keys(key):
    return jnp.clip(jax.random.normal(key, (SEQS, KVH, CACHE, HD), jnp.float32), -6.0, 6.0)


def draw_key_cache(key, part):
    base = shared_keys(key)
    return base.astype(jnp.bfloat16)


def draw_query(key, part):
    key = jax.random.fold_in(key, 5)
    entries = 3.0 * jnp.clip(jax.random.normal(key, (SEQS, HEADS, HD), jnp.float32), -4.0, 4.0)
    return entries.astype(jnp.bfloat16)


def draw_residual(key, part):
    key = jax.random.fold_in(key, 7)
    first, second = jax.random.split(key, 2)
    column = jnp.arange(D, dtype=jnp.float32) / D
    col_scale = 0.1 * jnp.exp(column * math.log(3.0)) * jnp.exp(jax.random.uniform(second, (D,), jnp.float32, 0.0, math.log(10.0)))
    values = jnp.clip(jax.random.normal(first, (SEQS, D), jnp.float32), -6.0, 6.0)
    return (values * col_scale[None, :]).astype(jnp.bfloat16)


def draw_lengths(key, part):
    key = jax.random.fold_in(key, 11)
    first, second = jax.random.split(key)
    drawn = jax.random.randint(first, (SEQS,), 2, CACHE + 1, dtype=jnp.int32)
    longest = jax.random.randint(second, (), 0, SEQS, dtype=jnp.int32)
    return jnp.where(jnp.arange(SEQS, dtype=jnp.int32) == longest, CACHE, drawn).astype(jnp.int32)


def strengthened(values, own_key, source, target, shards_of, factor):
    def block_of(axis_at):
        return (jnp.arange(values.shape[axis_at]) // (values.shape[axis_at] // shards_of)).reshape((-1,) + (1,) * (values.ndim - 1 - axis_at))

    first = jax.random.permutation(own_key, shards_of)[block_of(target)]
    second = (block_of(target) + shards_of // 2) % shards_of
    return jnp.where((block_of(source) == first) | (block_of(source) == second), factor * values, values)


def steps_of(rng, shape, cuts, least, high):
    gain = 1.0
    for position, shards_of in cuts:
        draws = jax.random.uniform(jax.random.fold_in(jax.random.fold_in(rng, 6), position), (shards_of,), jnp.float32, least / len(cuts), high / len(cuts))
        gain = gain * jnp.repeat(jnp.exp(draws), shape[position] // shards_of).reshape((-1,) + (1,) * (len(shape) - 1 - position))
    return gain


def scatter_about(stream_key, shape, spread, bound, shards=(), held_as=jnp.bfloat16):
    entries = spread * jax.random.normal(stream_key, shape, jnp.float32)
    if shards:
        entries = entries * steps_of(stream_key, shape, shards, -0.22, 0.18)
    return jnp.clip(entries, -bound, bound).astype(held_as)


def noise_with(rng, extent, spread, most, shards, heavy, held_as=jnp.bfloat16):
    values = spread * jax.random.normal(rng, extent, jnp.float32)
    if shards:
        values = values * steps_of(rng, extent, shards, -0.22, 0.18)
    return jnp.clip(strengthened(values, jax.random.fold_in(rng, 3), *heavy), -most, most).astype(held_as)


def setup_inputs(seed: int = 0) -> dict:
    keys = jax.random.split(jax.random.key(seed), 11)
    return {
        "query": draw_query(jax.random.fold_in(keys[10], 71), 0),
        "key_cache": draw_key_cache(jax.random.fold_in(keys[10], 71), 0),
        "value_cache": scatter_about(keys[2], (SEQS, KVH, CACHE, HD), 1.0, 6.0, ((1, 8), (2, 64))),
        "lengths": draw_lengths(jax.random.fold_in(keys[10], 71), 0),
        "residual": draw_residual(jax.random.fold_in(keys[10], 71), 0),
        "out_weight": scatter_about(keys[5], (HEADS * HD, D), (HEADS * HD) ** -0.5, 0.0625, ((0, 8), (1, 64))),
        "norm_gain": jnp.clip(1.0 + 0.15 * jax.random.normal(keys[6], (D,), jnp.float32), 0.25, 1.75).astype(jnp.bfloat16),
        "gate_weight": noise_with(keys[7], (D, FF), D ** -0.5, 0.1875, ((0, 64), (1, 8)), (0, 1, 64, 4.0)),
        "up_weight": noise_with(keys[8], (D, FF), D ** -0.5, 0.1875, ((0, 64), (1, 8)), (0, 1, 64, 4.0)),
        "down_weight": scatter_about(keys[9], (FF, D), FF ** -0.5, 0.03125, ((0, 8), (1, 64))),
    }


def reference(query, key_cache, value_cache, lengths, residual, out_weight, norm_gain, gate_weight, up_weight, down_weight):
    group_count = HEADS // KVH
    queries = query.astype(jnp.float32).reshape(SEQS, KVH, group_count, HD)
    keys_all = key_cache.astype(jnp.float32)
    values_all = value_cache.astype(jnp.float32)
    scores = jnp.einsum('skgd,sktd->skgt', queries, keys_all) / math.sqrt(HD)
    places = jnp.arange(CACHE, dtype=jnp.int32)
    is_live = (places[None, :] < lengths[:, None])[:, None, None, :]
    scores = jnp.where(is_live, scores, -1e+30)
    peak = lax.optimization_barrier(jnp.max(scores, axis=-1, keepdims=True))
    expo = jnp.where(is_live, jnp.exp(scores - peak), 0.0)
    total = lax.optimization_barrier(jnp.sum(expo, axis=-1))
    weights = expo.astype(jnp.bfloat16).astype(jnp.float32)
    numerator = jnp.einsum('skgt,sktd->skgd', weights, values_all)
    attended = (numerator / total[..., None]).reshape(SEQS, HEADS * HD).astype(jnp.bfloat16)
    projected = jnp.dot(attended, out_weight, preferred_element_type=jnp.float32)
    hidden_state = residual.astype(jnp.float32) + projected
    scale_row = lax.rsqrt(lax.optimization_barrier(jnp.mean(hidden_state * hidden_state, axis=1, keepdims=True)) + 1e-05)
    normed = (hidden_state * scale_row * norm_gain.astype(jnp.float32)).astype(jnp.bfloat16)
    gate = jnp.dot(normed, gate_weight, preferred_element_type=jnp.float32)
    upward = jnp.dot(normed, up_weight, preferred_element_type=jnp.float32)
    activated = (jax.nn.silu(gate) * upward).astype(jnp.bfloat16)
    downward = jnp.dot(activated, down_weight, preferred_element_type=jnp.float32)
    return (hidden_state + downward).astype(jnp.bfloat16)
```

```python
import math

import jax
import jax.numpy as jnp
from jax import lax
from jax.sharding import Mesh
from jax.sharding import PartitionSpec as P

KV = ("z", "x")
HEAD = ("y", "core")
NZ, NX, NY, NC = 16, 4, 4, 2
NEG = -1e30


def pieces(value):
    high = lax.reduce_precision(value, 8, 7)
    rest = value - high
    middle = lax.reduce_precision(rest, 8, 7)
    low = rest - middle
    return [high.astype(jnp.bfloat16), middle.astype(jnp.bfloat16), low.astype(jnp.bfloat16)]


def exchange(block, axis, count):
    return lax.all_to_all(jnp.broadcast_to(block[None], (count,) + block.shape), axis, 0, 0)


def merge(outs, logs, axis, count):
    rows = jnp.zeros((16, 128), jnp.bfloat16)
    rows = rows.at[0:3, 0:64].set(jnp.stack(pieces(logs)))
    got = exchange(jnp.concatenate([outs.astype(jnp.bfloat16), rows]), axis, count)
    logs = jnp.sum(got[:, 64:67, 0:64].astype(jnp.float32), axis=1)
    top = jnp.max(logs, axis=0)
    share = jnp.exp(logs - top)
    total = jnp.sum(share, axis=0)
    outs = jnp.sum(got[:, 0:64].astype(jnp.float32) * (share / total)[:, :, None], axis=0)
    return outs, top + jnp.log(total)


def local(
    query,
    key_cache,
    value_cache,
    lengths,
    residual,
    out_weight,
    norm_gain,
    gate_weight,
    up_weight,
    down_weight,
):
    batch_rows, _, block_len, head_size = key_cache.shape
    me = lax.axis_index(KV)
    scores = jnp.einsum(
        "sgd,std->sgt", query, key_cache[:, 0], preferred_element_type=jnp.float32
    ) / math.sqrt(head_size)
    places = me * block_len + lax.broadcasted_iota(jnp.int32, (batch_rows, block_len), 1)
    is_live = (places < lengths[:, None])[:, None, :]
    scores = jnp.where(is_live, scores, NEG)
    top = jnp.max(scores, axis=-1)
    expo = jnp.where(is_live, jnp.exp(scores - top[..., None]), 0.0)
    total = jnp.sum(expo, axis=-1)
    outs = jnp.einsum(
        "sgt,std->sgd",
        expo.astype(jnp.bfloat16),
        value_cache[:, 0],
        preferred_element_type=jnp.float32,
    )
    any_live = total > 0
    outs = outs / jnp.where(any_live, total, 1.0)[..., None]
    logs = jnp.where(any_live, top + jnp.log(jnp.where(any_live, total, 1.0)), NEG)
    outs, logs = outs.reshape(64, 128), logs.reshape(64)
    outs, logs = merge(outs, logs, "z", NZ)
    outs, logs = merge(outs, logs, "x", NX)
    attended = outs.reshape(batch_rows, 1024).astype(jnp.bfloat16)
    projected = jnp.dot(attended, out_weight, preferred_element_type=jnp.float32)
    projected = jnp.sum(exchange(projected, HEAD, NY * NC), axis=0)
    hidden_state = residual.astype(jnp.float32) + projected
    squares = jnp.sum(hidden_state * hidden_state, axis=1)
    scaled = (hidden_state * norm_gain.astype(jnp.float32)[None, :]).astype(jnp.bfloat16)
    gate = jnp.dot(scaled, gate_weight, preferred_element_type=jnp.float32)
    up = jnp.dot(scaled, up_weight, preferred_element_type=jnp.float32)
    tiles = jnp.concatenate([gate, up], axis=1).astype(jnp.bfloat16)
    tiles = tiles.reshape(batch_rows, 56, 128).transpose(1, 0, 2)
    extra = jnp.zeros((8, 8, 128), jnp.bfloat16)
    extra = extra.at[0, :, 0:3].set(jnp.stack(pieces(squares), axis=1))
    terms = lax.all_to_all(jnp.concatenate([tiles, extra]), KV, 0, 0)
    summed = jnp.sum(terms.astype(jnp.float32), axis=0)
    special = jnp.zeros((8, 128), jnp.bfloat16)
    special = special.at[:, 0:3].set(jnp.stack(pieces(jnp.sum(summed[:, 0:3], axis=1)), axis=1))
    got = exchange(jnp.where(me == 56, special, summed.astype(jnp.bfloat16)), KV, NZ * NX)
    squares = jnp.sum(got[56, :, 0:3].astype(jnp.float32), axis=1)
    scale_row = lax.rsqrt(squares / 8192 + 1e-05)
    whole = got[0:56].astype(jnp.float32) * scale_row[None, :, None]
    activated = (jax.nn.silu(whole[0:28]) * whole[28:56]).astype(jnp.bfloat16)
    activated = activated.transpose(1, 0, 2).reshape(batch_rows, 3584)
    downward = jnp.dot(activated, down_weight, preferred_element_type=jnp.float32)
    downward = jnp.sum(exchange(downward, HEAD, NY * NC), axis=0)
    return (hidden_state + downward).astype(jnp.bfloat16)


def solution(mesh):
    fine = Mesh(mesh.devices.reshape(NZ, NX, NY, NC), KV + HEAD)
    return jax.shard_map(
        local,
        mesh=fine,
        in_specs=(
            P(None, HEAD, None),
            P(None, HEAD, KV, None),
            P(None, HEAD, KV, None),
            P(),
            P(None, KV),
            P(HEAD, KV),
            P(KV),
            P(KV, HEAD),
            P(KV, HEAD),
            P(HEAD, KV),
        ),
        out_specs=P(None, KV),
        check_vma=False,
    )
```

```python
import math

import jax
import jax.numpy as jnp
from jax import lax
from jax.sharding import Mesh
from jax.sharding import PartitionSpec as P

NEAR = ("zl", "x")
FAR = "zh"
KV = ("zh", "zl", "x")
HEAD = ("y", "core")
SIZES = (8, 2, 4, 4, 2)
NEG = -1e30


def pieces(value):
    high = lax.reduce_precision(value, 8, 7)
    rest = value - high
    middle = lax.reduce_precision(rest, 8, 7)
    low = rest - middle
    return [high.astype(jnp.bfloat16), middle.astype(jnp.bfloat16), low.astype(jnp.bfloat16)]


def row_tile(value):
    return jnp.zeros((8, 128), jnp.bfloat16).at[:, 0:3].set(jnp.stack(pieces(value), axis=1))


def exchange(block, axis, count):
    return lax.all_to_all(jnp.broadcast_to(block[None], (count,) + block.shape), axis, 0, 0)


def merge(outs, logs, axis, count):
    rows = jnp.zeros((16, 128), jnp.bfloat16)
    rows = rows.at[0:3, 0:64].set(jnp.stack(pieces(logs)))
    got = exchange(jnp.concatenate([outs.astype(jnp.bfloat16), rows]), axis, count)
    logs = jnp.sum(got[:, 64:67, 0:64].astype(jnp.float32), axis=1)
    top = jnp.max(logs, axis=0)
    share = jnp.exp(logs - top)
    total = jnp.sum(share, axis=0)
    outs = jnp.sum(got[:, 0:64].astype(jnp.float32) * (share / total)[:, :, None], axis=0)
    return outs, top + jnp.log(total)


def local(
    query,
    key_cache,
    value_cache,
    lengths,
    residual,
    out_weight,
    norm_gain,
    gate_weight,
    up_weight,
    down_weight,
):
    batch_rows, _, block_len, head_size = key_cache.shape
    me = lax.axis_index(KV)
    scores = jnp.einsum(
        "sgd,std->sgt", query, key_cache[:, 0], preferred_element_type=jnp.float32
    ) / math.sqrt(head_size)
    places = me * block_len + lax.broadcasted_iota(jnp.int32, (batch_rows, block_len), 1)
    is_live = (places < lengths[:, None])[:, None, :]
    scores = jnp.where(is_live, scores, NEG)
    top = jnp.max(scores, axis=-1)
    expo = jnp.where(is_live, jnp.exp(scores - top[..., None]), 0.0)
    total = jnp.sum(expo, axis=-1)
    outs = jnp.einsum(
        "sgt,std->sgd",
        expo.astype(jnp.bfloat16),
        value_cache[:, 0],
        preferred_element_type=jnp.float32,
    )
    any_live = total > 0
    outs = outs / jnp.where(any_live, total, 1.0)[..., None]
    logs = jnp.where(any_live, top + jnp.log(jnp.where(any_live, total, 1.0)), NEG)
    outs, logs = outs.reshape(64, 128), logs.reshape(64)
    outs, logs = merge(outs, logs, NEAR, 8)
    outs, logs = merge(outs, logs, FAR, 8)
    attended = outs.reshape(batch_rows, 1024).astype(jnp.bfloat16)
    projected = jnp.dot(attended, out_weight, preferred_element_type=jnp.float32)
    gain = norm_gain.astype(jnp.float32)[None, :]
    projected, gain = lax.optimization_barrier((projected, gain))
    projected = jnp.sum(exchange(projected, HEAD, 8), axis=0)
    hidden_state = residual.astype(jnp.float32) + projected
    squares = jnp.sum(hidden_state * hidden_state, axis=1)
    scaled = (hidden_state * gain).astype(jnp.bfloat16)
    gate = jnp.dot(scaled, gate_weight, preferred_element_type=jnp.float32)
    up = jnp.dot(scaled, up_weight, preferred_element_type=jnp.float32)
    tiles = jnp.concatenate([gate, up], axis=1).astype(jnp.bfloat16)
    tiles = tiles.reshape(batch_rows, 8, 7, 128).transpose(1, 2, 0, 3)
    extra = jnp.broadcast_to(row_tile(squares)[None, None], (8, 1, 8, 128))
    packed = jnp.concatenate([tiles, extra], axis=1)
    packed, hidden_state = lax.optimization_barrier((packed, hidden_state))
    terms = lax.all_to_all(packed, NEAR, 0, 0)
    summed = jnp.sum(terms.astype(jnp.float32), axis=0)
    squares = jnp.sum(summed[7, :, 0:3], axis=1)
    packed = jnp.concatenate([summed[0:7].astype(jnp.bfloat16), row_tile(squares)[None]])
    terms = exchange(packed, FAR, 8)
    summed = jnp.sum(terms.astype(jnp.float32), axis=0)
    squares = jnp.sum(summed[7, :, 0:3], axis=1)
    scale_row = lax.rsqrt(squares / 8192 + 1e-05)
    whole = (summed[0:7] * scale_row[None, :, None]).astype(jnp.bfloat16)
    whole = exchange(whole, NEAR, 8).reshape(56, 8, 128).astype(jnp.float32)
    activated = (jax.nn.silu(whole[0:28]) * whole[28:56]).astype(jnp.bfloat16)
    activated = activated.transpose(1, 0, 2).reshape(batch_rows, 3584)
    downward = jnp.dot(activated, down_weight, preferred_element_type=jnp.float32)
    downward = jnp.sum(exchange(downward, HEAD, 8), axis=0)
    return (hidden_state + downward).astype(jnp.bfloat16)


def solution(mesh):
    fine = Mesh(mesh.devices.reshape(SIZES), KV + HEAD)
    return jax.shard_map(
        local,
        mesh=fine,
        in_specs=(
            P(None, HEAD, None),
            P(None, HEAD, KV, None),
            P(None, HEAD, KV, None),
            P(),
            P(None, KV),
            P(HEAD, KV),
            P(KV),
            P(KV, HEAD),
            P(KV, HEAD),
            P(HEAD, KV),
        ),
        out_specs=P(None, KV),
        check_vma=False,
    )
```

```python
import math

import jax
import jax.numpy as jnp
from jax import lax
from jax.experimental import pallas as pl
from jax.experimental.pallas import tpu as pltpu
from jax.sharding import Mesh
from jax.sharding import PartitionSpec as P

NEAR = ("zl", "x")
FAR = "zh"
KV = ("zh", "zl", "x")
HEAD = ("y", "core")
SIZES = (8, 2, 4, 4, 2)
NEG = -1e30


def pieces(value, masks):
    high = lax.reduce_precision(value, 8, 7)
    middle = lax.reduce_precision(value - high, 8, 7)
    low = value - high - middle
    return (high * masks[0] + middle * masks[1] + low * masks[2]).astype(jnp.bfloat16)


def attend(
    query, keys, values, lengths, gain, packed, row_masks, lane_masks, gain_out,
    q_buf, k_buf, v_buf, l_buf, g_buf, s_sem,
):
    rows, _, block_len, _ = k_buf.shape
    small = [
        pltpu.make_async_copy(lengths, l_buf, s_sem.at[0]),
        pltpu.make_async_copy(query, q_buf, s_sem.at[1]),
        pltpu.make_async_copy(gain, g_buf, s_sem.at[2]),
    ]
    k_in = pltpu.make_async_copy(keys, k_buf, s_sem.at[3])
    v_in = pltpu.make_async_copy(values, v_buf, s_sem.at[4])
    for copy in small + [k_in, v_in]:
        copy.start()
    wide = (16, 128)
    row, lane = lax.broadcasted_iota(jnp.int32, wide, 0), lax.broadcasted_iota(jnp.int32, wide, 1)
    one, zero = jnp.float32(1), jnp.float32(0)
    for i in range(3):
        row_masks[i] = jnp.where(row == i, one, zero)
        lane_masks[i] = jnp.where(lane[0:8] == i, one, zero)
    first = lax.axis_index(KV) * block_len
    place = first + lax.broadcasted_iota(jnp.int32, (8, block_len), 1)
    for copy in small:
        copy.wait()
    gain_out[...] = jnp.broadcast_to(g_buf[...].astype(jnp.float32), (8, 128))
    scores, live = [], []
    k_in.wait()
    for s in range(rows):
        product = lax.dot_general(
            q_buf[s], k_buf[s, 0], (((1,), (1,)), ((), ())), preferred_element_type=jnp.float32
        )
        scores.append(product * (1.0 / math.sqrt(128)))
        live.append(place < l_buf[s])
    tops, totals, expos = [], [], []
    for s in range(rows):
        masked = jnp.where(live[s], scores[s], NEG)
        top = jnp.max(masked, axis=1, keepdims=True)
        expo = jnp.where(live[s], jnp.exp(masked - top), 0.0)
        tops.append(top)
        totals.append(jnp.sum(expo, axis=1, keepdims=True))
        expos.append(expo.astype(jnp.bfloat16))
    outs, logs = [], jnp.zeros((8, 128), jnp.float32)
    sub = row[0:8]
    v_in.wait()
    for s in range(rows):
        some = totals[s] > 0
        total = jnp.where(some, totals[s], 1.0)
        log = jnp.where(some, tops[s] + jnp.log(total), NEG)
        logs = logs + jnp.where(lane[0:8] == sub + 8 * s, jnp.broadcast_to(log, (8, 128)), 0.0)
        out = jnp.dot(expos[s], v_buf[s, 0], preferred_element_type=jnp.float32)
        outs.append(out / total)
    logs = jnp.broadcast_to(jnp.sum(logs, axis=0, keepdims=True), wide)
    high = logs.astype(jnp.bfloat16).astype(jnp.float32)
    middle = (logs - high).astype(jnp.bfloat16).astype(jnp.float32)
    low = logs - high - middle
    tail = jnp.where(row == 0, high, jnp.where(row == 1, middle, jnp.where(row == 2, low, 0.0)))
    block = jnp.concatenate(outs + [tail], axis=0).astype(jnp.bfloat16)
    for d in range(8):
        packed[d] = block


def attention(query, keys, values, lengths, gain):
    f32, bf16 = jnp.float32, jnp.bfloat16
    whole = pl.BlockSpec(memory_space=pltpu.VMEM)
    return pl.pallas_call(
        attend,
        out_shape=(
            pltpu.VMEM((8, 80, 128), bf16),
            pltpu.VMEM((3, 16, 128), f32),
            pltpu.VMEM((3, 8, 128), f32),
            pltpu.VMEM((8, 128), f32),
        ),
        in_specs=[pl.BlockSpec(memory_space=pl.ANY)] * 5,
        out_specs=(whole,) * 4,
        scratch_shapes=[
            pltpu.VMEM(query.shape, bf16),
            pltpu.VMEM(keys.shape, bf16),
            pltpu.VMEM(values.shape, bf16),
            pltpu.SMEM(lengths.shape, jnp.int32),
            pltpu.VMEM((1, 128), bf16),
            pltpu.SemaphoreType.DMA((5,)),
        ],
        compiler_params=pltpu.CompilerParams(vmem_limit_bytes=60 * 2**20),
        name="attention",
    )(query, keys, values, lengths, gain.reshape(1, 128))


def exchange(block, axis, count):
    return lax.all_to_all(jnp.broadcast_to(block[None], (count,) + block.shape), axis, 0, 0)


def merge(got):
    logs = jnp.sum(got[:, 64:80, 0:64].astype(jnp.float32), axis=1)
    top = jnp.max(logs, axis=0)
    share = jnp.exp(logs - top)
    total = jnp.sum(share, axis=0)
    outs = jnp.sum(got[:, 0:64].astype(jnp.float32) * (share / total)[:, :, None], axis=0)
    return outs.astype(jnp.bfloat16), top + jnp.log(total)


def local(
    query,
    key_cache,
    value_cache,
    lengths,
    residual,
    out_weight,
    norm_gain,
    gate_weight,
    up_weight,
    down_weight,
):
    packed, row_masks, lane_masks, gain = attention(
        query, key_cache, value_cache, lengths, norm_gain
    )
    outs, logs = merge(lax.all_to_all(packed, NEAR, 0, 0))
    tail = pieces(jnp.broadcast_to(jnp.concatenate([logs, logs])[None], (16, 128)), row_masks)
    outs, _ = merge(exchange(jnp.concatenate([outs, tail]), FAR, 8))
    attended = outs.reshape(8, 1024)
    projected = jnp.dot(attended, out_weight, preferred_element_type=jnp.float32)
    projected = jnp.sum(exchange(projected, HEAD, 8), axis=0)
    hidden_state = residual.astype(jnp.float32) + projected
    squares = jnp.sum(hidden_state * hidden_state, axis=1, keepdims=True)
    scaled = (hidden_state * gain).astype(jnp.bfloat16)
    gate = jnp.dot(scaled, gate_weight, preferred_element_type=jnp.float32)
    up = jnp.dot(scaled, up_weight, preferred_element_type=jnp.float32)
    tiles = jnp.concatenate([gate, up], axis=1).astype(jnp.bfloat16)
    tiles = tiles.reshape(8, 8, 7, 128).transpose(1, 2, 0, 3)
    extra = jnp.broadcast_to(pieces(jnp.broadcast_to(squares, (8, 128)), lane_masks)[None, None], (8, 1, 8, 128))
    packed = jnp.concatenate([tiles, extra], axis=1)
    packed, hidden_state = lax.optimization_barrier((packed, hidden_state))
    terms = lax.all_to_all(packed, NEAR, 0, 0)
    summed = jnp.sum(terms.astype(jnp.float32), axis=0)
    squares = jnp.sum(summed[7], axis=1, keepdims=True)
    packed = jnp.concatenate([summed[0:7].astype(jnp.bfloat16), pieces(jnp.broadcast_to(squares, (8, 128)), lane_masks)[None]])
    terms = exchange(packed, FAR, 8)
    summed = jnp.sum(terms.astype(jnp.float32), axis=0)
    squares = jnp.sum(summed[7], axis=1, keepdims=True)
    scale_row = lax.rsqrt(squares / 8192 + 1e-05)
    whole = (summed[0:7] * scale_row[None]).astype(jnp.bfloat16)
    whole = exchange(whole, NEAR, 8).reshape(56, 8, 128).astype(jnp.float32)
    activated = (jax.nn.silu(whole[0:28]) * whole[28:56]).astype(jnp.bfloat16)
    activated = activated.transpose(1, 0, 2).reshape(8, 3584)
    downward = jnp.dot(activated, down_weight, preferred_element_type=jnp.float32)
    downward = jnp.sum(exchange(downward, HEAD, 8), axis=0)
    return (hidden_state + downward).astype(jnp.bfloat16)


def solution(mesh):
    fine = Mesh(mesh.devices.reshape(SIZES), KV + HEAD)
    return jax.shard_map(
        local,
        mesh=fine,
        in_specs=(
            P(None, HEAD, None),
            P(None, HEAD, KV, None),
            P(None, HEAD, KV, None),
            P(),
            P(None, KV),
            P(HEAD, KV),
            P(KV),
            P(KV, HEAD),
            P(KV, HEAD),
            P(HEAD, KV),
        ),
        out_specs=P(None, KV),
        check_vma=False,
    )
```

```python
import math

import jax
import jax.numpy as jnp
from jax import lax
from jax.experimental import pallas as pl
from jax.experimental.pallas import tpu as pltpu
from jax.sharding import Mesh
from jax.sharding import PartitionSpec as P

KV = ("z", "x")
HEAD = ("y", "core")
SIZES = (16, 4, 4, 2)
FAR = [[2 * pair + (pair // 4 + half) % 2 for pair in range(8)] for half in range(2)]
NEAR = [[FAR[half][pair] * 4 + x for half in range(2) for x in range(4)] for pair in range(8)]
NEG = -1e30


def pieces(value, masks):
    high = lax.reduce_precision(value, 8, 7)
    middle = lax.reduce_precision(value - high, 8, 7)
    low = value - high - middle
    return (high * masks[0] + middle * masks[1] + low * masks[2]).astype(jnp.bfloat16)


def attend(
    query, keys, values, lengths, gain, packed, row_masks, lane_masks, gain_out,
    q_buf, k_buf, v_buf, l_buf, g_buf, s_sem,
):
    rows, _, block_len, _ = k_buf.shape
    small = [
        pltpu.make_async_copy(lengths, l_buf, s_sem.at[0]),
        pltpu.make_async_copy(query, q_buf, s_sem.at[1]),
        pltpu.make_async_copy(gain, g_buf, s_sem.at[2]),
    ]
    k_in = pltpu.make_async_copy(keys, k_buf, s_sem.at[3])
    v_in = pltpu.make_async_copy(values, v_buf, s_sem.at[4])
    for copy in small + [k_in, v_in]:
        copy.start()
    wide = (8, 128)
    row, lane = lax.broadcasted_iota(jnp.int32, wide, 0), lax.broadcasted_iota(jnp.int32, wide, 1)
    one, zero = jnp.float32(1), jnp.float32(0)
    for i in range(3):
        row_masks[i] = jnp.where(row == i, one, zero)
        lane_masks[i] = jnp.where(lane == i, one, zero)
    first = lax.axis_index(KV) * block_len
    place = first + lax.broadcasted_iota(jnp.int32, (8, block_len), 1)
    for copy in small:
        copy.wait()
    gain_out[...] = jnp.broadcast_to(g_buf[...].astype(jnp.float32), (8, 128))
    scores, live = [], []
    k_in.wait()
    for s in range(rows):
        product = lax.dot_general(
            q_buf[s], k_buf[s, 0], (((1,), (1,)), ((), ())), preferred_element_type=jnp.float32
        )
        scores.append(product * (1.0 / math.sqrt(128)))
        live.append(place < l_buf[s])
    tops, totals, expos = [], [], []
    for s in range(rows):
        masked = jnp.where(live[s], scores[s], NEG)
        top = jnp.max(masked, axis=1, keepdims=True)
        expo = jnp.where(live[s], jnp.exp(masked - top), 0.0)
        tops.append(top)
        totals.append(jnp.sum(expo, axis=1, keepdims=True))
        expos.append(expo.astype(jnp.bfloat16))
    outs, logs = [], jnp.zeros((8, 128), jnp.float32)
    v_in.wait()
    for s in range(rows):
        some = totals[s] > 0
        total = jnp.where(some, totals[s], 1.0)
        log = jnp.where(some, tops[s] + jnp.log(total), NEG)
        logs = logs + jnp.where(lane == row + 8 * s, jnp.broadcast_to(log, (8, 128)), 0.0)
        out = jnp.dot(expos[s], v_buf[s, 0], preferred_element_type=jnp.float32)
        outs.append(out / total)
    logs = jnp.broadcast_to(jnp.sum(logs, axis=0, keepdims=True), wide)
    high = logs.astype(jnp.bfloat16).astype(jnp.float32)
    middle = (logs - high).astype(jnp.bfloat16).astype(jnp.float32)
    low = logs - high - middle
    tail = jnp.where(row == 0, high, jnp.where(row == 1, middle, jnp.where(row == 2, low, 0.0)))
    block = jnp.concatenate(outs + [tail], axis=0).astype(jnp.bfloat16)
    for d in range(8):
        packed[d] = block


def attention(query, keys, values, lengths, gain):
    f32, bf16 = jnp.float32, jnp.bfloat16
    whole = pl.BlockSpec(memory_space=pltpu.VMEM)
    return pl.pallas_call(
        attend,
        out_shape=(
            pltpu.VMEM((8, 72, 128), bf16),
            pltpu.VMEM((3, 8, 128), f32),
            pltpu.VMEM((3, 8, 128), f32),
            pltpu.VMEM((8, 128), f32),
        ),
        in_specs=[pl.BlockSpec(memory_space=pl.ANY)] * 5,
        out_specs=(whole,) * 4,
        scratch_shapes=[
            pltpu.VMEM(query.shape, bf16),
            pltpu.VMEM(keys.shape, bf16),
            pltpu.VMEM(values.shape, bf16),
            pltpu.SMEM(lengths.shape, jnp.int32),
            pltpu.VMEM((1, 128), bf16),
            pltpu.SemaphoreType.DMA((5,)),
        ],
        compiler_params=pltpu.CompilerParams(vmem_limit_bytes=60 * 2**20),
        name="attention",
    )(query, keys, values, lengths, gain.reshape(1, 128))


def near(blocks):
    return lax.all_to_all(blocks, KV, 0, 0, axis_index_groups=NEAR)


def far(blocks):
    return lax.all_to_all(blocks, "z", 0, 0, axis_index_groups=FAR)


def heads(blocks):
    return lax.all_to_all(blocks, HEAD, 0, 0)


def spread(block):
    return jnp.broadcast_to(block[None], (8,) + block.shape)


def merge(got):
    logs = jnp.sum(got[:, 64:72, 0:64].astype(jnp.float32), axis=1)
    top = jnp.max(logs, axis=0)
    share = jnp.exp(logs - top)
    total = jnp.sum(share, axis=0)
    outs = jnp.sum(got[:, 0:64].astype(jnp.float32) * (share / total)[:, :, None], axis=0)
    return outs.astype(jnp.bfloat16), top + jnp.log(total)


def local(
    query,
    key_cache,
    value_cache,
    lengths,
    residual,
    out_weight,
    norm_gain,
    gate_weight,
    up_weight,
    down_weight,
):
    packed, row_masks, lane_masks, gain = attention(
        query, key_cache, value_cache, lengths, norm_gain
    )
    outs, logs = merge(near(packed))
    tail = pieces(jnp.broadcast_to(jnp.concatenate([logs, logs])[None], (8, 128)), row_masks)
    outs, _ = merge(far(spread(jnp.concatenate([outs, tail]))))
    attended = outs.reshape(8, 1024)
    projected = jnp.dot(attended, out_weight, preferred_element_type=jnp.float32)
    projected = jnp.sum(heads(spread(projected)), axis=0)
    hidden_state = residual.astype(jnp.float32) + projected
    squares = jnp.sum(hidden_state * hidden_state, axis=1, keepdims=True)
    scaled = (hidden_state * gain).astype(jnp.bfloat16)
    gate = jnp.dot(scaled, gate_weight, preferred_element_type=jnp.float32)
    up = jnp.dot(scaled, up_weight, preferred_element_type=jnp.float32)
    tiles = jnp.concatenate([gate, up], axis=1).astype(jnp.bfloat16)
    tiles = tiles.reshape(8, 8, 7, 128).transpose(1, 2, 0, 3)
    extra = jnp.broadcast_to(pieces(jnp.broadcast_to(squares, (8, 128)), lane_masks)[None, None], (8, 1, 8, 128))
    packed = jnp.concatenate([tiles, extra], axis=1)
    packed, hidden_state = lax.optimization_barrier((packed, hidden_state))
    terms = near(packed)
    summed = jnp.sum(terms.astype(jnp.float32), axis=0)
    squares = jnp.sum(summed[7], axis=1, keepdims=True)
    packed = jnp.concatenate([summed[0:7].astype(jnp.bfloat16), pieces(jnp.broadcast_to(squares, (8, 128)), lane_masks)[None]])
    terms = far(spread(packed))
    summed = jnp.sum(terms.astype(jnp.float32), axis=0)
    squares = jnp.sum(summed[7], axis=1, keepdims=True)
    scale_row = lax.rsqrt(squares / 8192 + 1e-05)
    whole = (summed[0:7] * scale_row[None]).astype(jnp.bfloat16)
    whole = near(spread(whole)).reshape(56, 8, 128).astype(jnp.float32)
    activated = (jax.nn.silu(whole[0:28]) * whole[28:56]).astype(jnp.bfloat16)
    activated = activated.transpose(1, 0, 2).reshape(8, 3584)
    downward = jnp.dot(activated, down_weight, preferred_element_type=jnp.float32)
    downward = jnp.sum(heads(spread(downward)), axis=0)
    return (hidden_state + downward).astype(jnp.bfloat16)


def solution(mesh):
    fine = Mesh(mesh.devices.reshape(SIZES), KV + HEAD)
    return jax.shard_map(
        local,
        mesh=fine,
        in_specs=(
            P(None, HEAD, None),
            P(None, HEAD, KV, None),
            P(None, HEAD, KV, None),
            P(),
            P(None, KV),
            P(HEAD, KV),
            P(KV),
            P(KV, HEAD),
            P(KV, HEAD),
            P(HEAD, KV),
        ),
        out_specs=P(None, KV),
        check_vma=False,
    )
```

```python
import math

import jax
import jax.numpy as jnp
from jax import lax
from jax.experimental import pallas as pl
from jax.experimental.pallas import tpu as pltpu
from jax.sharding import Mesh
from jax.sharding import PartitionSpec as P

KV = ("z", "x")
HEAD = ("y", "core")
SIZES = (16, 4, 4, 2)
FAR = [[2 * pair + (pair // 4 + half) % 2 for pair in range(8)] for half in range(2)]
NEAR = [[FAR[half][pair] * 4 + x for half in range(2) for x in range(4)] for pair in range(8)]
NEG = -1e30


def attend(
    query, keys, values, lengths, gain, packed, gain_out,
    q_buf, k_buf, v_buf, l_buf, g_buf, s_sem,
):
    rows, _, block_len, _ = k_buf.shape
    small = [
        pltpu.make_async_copy(lengths, l_buf, s_sem.at[0]),
        pltpu.make_async_copy(query, q_buf, s_sem.at[1]),
        pltpu.make_async_copy(gain, g_buf, s_sem.at[2]),
    ]
    k_in = pltpu.make_async_copy(keys, k_buf, s_sem.at[3])
    v_in = pltpu.make_async_copy(values, v_buf, s_sem.at[4])
    for copy in small + [k_in, v_in]:
        copy.start()
    wide = (8, 128)
    row, lane = lax.broadcasted_iota(jnp.int32, wide, 0), lax.broadcasted_iota(jnp.int32, wide, 1)
    first = lax.axis_index(KV) * block_len
    place = first + lax.broadcasted_iota(jnp.int32, (8, block_len), 1)
    for copy in small:
        copy.wait()
    gain_out[...] = jnp.broadcast_to(g_buf[...].astype(jnp.float32), (8, 128))
    scores, live = [], []
    k_in.wait()
    for s in range(rows):
        product = lax.dot_general(
            q_buf[s], k_buf[s, 0], (((1,), (1,)), ((), ())), preferred_element_type=jnp.float32
        )
        scores.append(product * (1.0 / math.sqrt(128)))
        live.append(place < l_buf[s])
    tops, totals, expos = [], [], []
    for s in range(rows):
        masked = jnp.where(live[s], scores[s], NEG)
        top = jnp.max(masked, axis=1, keepdims=True)
        expo = jnp.where(live[s], jnp.exp(masked - top), 0.0)
        tops.append(top)
        totals.append(jnp.sum(expo, axis=1, keepdims=True))
        expos.append(expo.astype(jnp.bfloat16))
    outs, logs = [], jnp.zeros((8, 128), jnp.float32)
    v_in.wait()
    for s in range(rows):
        some = totals[s] > 0
        total = jnp.where(some, totals[s], 1.0)
        log = jnp.where(some, tops[s] + jnp.log(total), NEG)
        logs = logs + jnp.where(lane == row + 8 * s, jnp.broadcast_to(log, (8, 128)), 0.0)
        out = jnp.dot(expos[s], v_buf[s, 0], preferred_element_type=jnp.float32)
        outs.append(out / total)
    tail = tail_of(jnp.sum(logs, axis=0, keepdims=True))
    block = jnp.concatenate(outs + [tail], axis=0).astype(jnp.bfloat16)
    for d in range(8):
        packed[d] = block


def attention(query, keys, values, lengths, gain):
    f32, bf16 = jnp.float32, jnp.bfloat16
    whole = pl.BlockSpec(memory_space=pltpu.VMEM)
    return pl.pallas_call(
        attend,
        out_shape=(
            pltpu.VMEM((8, 72, 128), bf16),
            pltpu.VMEM((8, 128), f32),
        ),
        in_specs=[pl.BlockSpec(memory_space=pl.ANY)] * 5,
        out_specs=(whole,) * 2,
        scratch_shapes=[
            pltpu.VMEM(query.shape, bf16),
            pltpu.VMEM(keys.shape, bf16),
            pltpu.VMEM(values.shape, bf16),
            pltpu.SMEM(lengths.shape, jnp.int32),
            pltpu.VMEM((1, 128), bf16),
            pltpu.SemaphoreType.DMA((5,)),
        ],
        compiler_params=pltpu.CompilerParams(vmem_limit_bytes=60 * 2**20),
        name="attention",
    )(query, keys, values, lengths, gain.reshape(1, 128))


def near(blocks):
    return lax.all_to_all(blocks, KV, 0, 0, axis_index_groups=NEAR)


def far(blocks):
    return lax.all_to_all(blocks, "z", 0, 0, axis_index_groups=FAR)


def heads(blocks):
    return lax.all_to_all(blocks, HEAD, 0, 0)


def spread(block):
    return jnp.broadcast_to(block[None], (8,) + block.shape)


def tail_of(logs):
    row = lax.broadcasted_iota(jnp.int32, (8, 128), 0)
    logs = jnp.broadcast_to(logs, (8, 128))
    high = logs.astype(jnp.bfloat16).astype(jnp.float32)
    middle = (logs - high).astype(jnp.bfloat16).astype(jnp.float32)
    low = logs - high - middle
    return jnp.where(row == 0, high, jnp.where(row == 1, middle, jnp.where(row == 2, low, 0.0)))


def merged(got):
    parts = [got[i].astype(jnp.float32) for i in range(8)]
    logs = jnp.concatenate([jnp.sum(p[64:72], axis=0, keepdims=True) for p in parts], axis=0)
    top = jnp.max(logs, axis=0, keepdims=True)
    share = jnp.exp(logs - top)
    total = jnp.sum(share, axis=0, keepdims=True)
    weights = jnp.transpose(share / total)
    outs = parts[0][0:64] * weights[0:64, 0:1]
    for i in range(1, 8):
        outs = outs + parts[i][0:64] * weights[0:64, i : i + 1]
    return outs, top + jnp.log(total)


def merge_near(got, packed):
    outs, logs = merged(got)
    block = jnp.concatenate([outs, tail_of(logs)], axis=0).astype(jnp.bfloat16)
    for i in range(8):
        packed[i] = block


def merge_far(got, out):
    out[...] = merged(got)[0].astype(jnp.bfloat16)


def summed(terms):
    total = terms[0].astype(jnp.float32)
    for i in range(1, 8):
        total = total + terms[i].astype(jnp.float32)
    return total, jnp.sum(total[7], axis=1, keepdims=True)


def row_tile(value):
    lane = lax.broadcasted_iota(jnp.int32, (8, 128), 1)
    value = jnp.broadcast_to(value, (8, 128))
    high = value.astype(jnp.bfloat16).astype(jnp.float32)
    middle = (value - high).astype(jnp.bfloat16).astype(jnp.float32)
    low = value - high - middle
    return jnp.where(lane == 0, high, jnp.where(lane == 1, middle, jnp.where(lane == 2, low, 0.0)))


def gate_up(terms, residual, gain, gate_weight, up_weight, hidden_out, packed):
    hidden = residual[...].astype(jnp.float32)
    projected = terms[0]
    for i in range(1, 8):
        projected = projected + terms[i]
    hidden = hidden + projected
    hidden_out[...] = hidden
    scaled = (hidden * gain[...]).astype(jnp.bfloat16)
    tile = row_tile(jnp.sum(hidden * hidden, axis=1, keepdims=True)).astype(jnp.bfloat16)
    for i in range(8):
        packed[i, 7] = tile
    for first, weight in ((0, gate_weight), (28, up_weight)):
        product = jnp.dot(scaled, weight[...], preferred_element_type=jnp.float32)
        for t in range(28):
            place = first + t
            packed[place // 7, place % 7] = product[:, 128 * t : 128 * t + 128].astype(jnp.bfloat16)


def sum_near(terms, packed):
    total, squares = summed(terms)
    block = jnp.concatenate([total[0:7], row_tile(squares)[None]], axis=0).astype(jnp.bfloat16)
    for i in range(8):
        packed[i] = block


def sum_far(terms, packed):
    total, squares = summed(terms)
    block = (total[0:7] * lax.rsqrt(squares / 8192 + 1e-05)[None]).astype(jnp.bfloat16)
    for i in range(8):
        packed[i] = block


def step(body, shapes, count=1):
    whole = pl.BlockSpec(memory_space=pltpu.VMEM)
    return pl.pallas_call(
        body,
        out_shape=tuple(pltpu.VMEM(shape, dtype) for shape, dtype in shapes),
        in_specs=[whole] * count,
        out_specs=(whole,) * len(shapes),
        compiler_params=pltpu.CompilerParams(vmem_limit_bytes=4 * 2**20),
        name=body.__name__,
    )


def local(
    query,
    key_cache,
    value_cache,
    lengths,
    residual,
    out_weight,
    norm_gain,
    gate_weight,
    up_weight,
    down_weight,
):
    f32, bf16 = jnp.float32, jnp.bfloat16
    packed, gain = attention(query, key_cache, value_cache, lengths, norm_gain)
    (packed,) = step(merge_near, [((8, 72, 128), bf16)])(near(packed))
    (outs,) = step(merge_far, [((64, 128), bf16)])(far(packed))
    attended = outs.reshape(8, 1024)
    projected = jnp.dot(attended, out_weight, preferred_element_type=f32)
    hidden_state, packed = step(gate_up, [((8, 128), f32), ((8, 8, 8, 128), bf16)], 5)(
        heads(spread(projected)), residual, gain, gate_weight, up_weight
    )
    (packed,) = step(sum_near, [((8, 8, 8, 128), bf16)])(near(packed))
    (packed,) = step(sum_far, [((8, 7, 8, 128), bf16)])(far(packed))
    whole = near(packed).reshape(56, 8, 128).astype(jnp.float32)
    activated = (jax.nn.silu(whole[0:28]) * whole[28:56]).astype(jnp.bfloat16)
    activated = activated.transpose(1, 0, 2).reshape(8, 3584)
    downward = jnp.dot(activated, down_weight, preferred_element_type=jnp.float32)
    downward = jnp.sum(heads(spread(downward)), axis=0)
    return (hidden_state + downward).astype(jnp.bfloat16)


def solution(mesh):
    fine = Mesh(mesh.devices.reshape(SIZES), KV + HEAD)
    return jax.shard_map(
        local,
        mesh=fine,
        in_specs=(
            P(None, HEAD, None),
            P(None, HEAD, KV, None),
            P(None, HEAD, KV, None),
            P(),
            P(None, KV),
            P(HEAD, KV),
            P(KV),
            P(KV, HEAD),
            P(KV, HEAD),
            P(HEAD, KV),
        ),
        out_specs=P(None, KV),
        check_vma=False,
    )
```

```python
import math

import jax
import jax.numpy as jnp
from jax import lax
from jax.experimental import pallas as pl
from jax.experimental.pallas import tpu as pltpu
from jax.sharding import Mesh
from jax.sharding import PartitionSpec as P

KV = ("z", "x")
HEAD = ("y", "core")
SIZES = (16, 4, 4, 2)
FAR = [[2 * pair + (pair // 4 + half) % 2 for pair in range(8)] for half in range(2)]
NEAR = [[FAR[half][pair] * 4 + x for half in range(2) for x in range(4)] for pair in range(8)]
FAR = [[members[pair] for pair in (4, 3, 5, 2, 6, 1, 7, 0)] for members in FAR]
NEG = -1e30


def attend(
    query, keys, values, lengths, gain, packed, gain_out,
    q_buf, k_buf, v_buf, l_buf, g_buf, s_sem,
):
    rows, _, block_len, _ = k_buf.shape
    small = [
        pltpu.make_async_copy(lengths, l_buf, s_sem.at[0]),
        pltpu.make_async_copy(query, q_buf, s_sem.at[1]),
        pltpu.make_async_copy(gain, g_buf, s_sem.at[2]),
    ]
    k_in = pltpu.make_async_copy(keys, k_buf, s_sem.at[3])
    v_in = pltpu.make_async_copy(values, v_buf, s_sem.at[4])
    for copy in small[0:2] + [k_in, v_in, small[2]]:
        copy.start()
    wide = (8, 128)
    row, lane = lax.broadcasted_iota(jnp.int32, wide, 0), lax.broadcasted_iota(jnp.int32, wide, 1)
    first = lax.axis_index(KV) * block_len
    place = first + lax.broadcasted_iota(jnp.int32, (8, block_len), 1)
    for copy in small:
        copy.wait()
    gain_out[...] = jnp.broadcast_to(g_buf[...].astype(jnp.float32), (8, 128))
    scores, live = [], []
    k_in.wait()
    for s in range(rows):
        product = lax.dot_general(
            q_buf[s], k_buf[s, 0], (((1,), (1,)), ((), ())), preferred_element_type=jnp.float32
        )
        scores.append(product * (1.0 / math.sqrt(128)))
        live.append(place < l_buf[s])
    tops, totals, expos = [], [], []
    for s in range(rows):
        masked = jnp.where(live[s], scores[s], NEG)
        top = jnp.max(masked, axis=1, keepdims=True)
        expo = jnp.where(live[s], jnp.exp(masked - top), 0.0)
        tops.append(top)
        totals.append(jnp.sum(expo, axis=1, keepdims=True))
        expos.append(expo.astype(jnp.bfloat16))
    outs, logs = [], jnp.zeros((8, 128), jnp.float32)
    v_in.wait()
    for s in range(rows):
        some = totals[s] > 0
        total = jnp.where(some, totals[s], 1.0)
        log = jnp.where(some, tops[s] + jnp.log(total), NEG)
        logs = logs + jnp.where(lane == row + 8 * s, jnp.broadcast_to(log, (8, 128)), 0.0)
        out = jnp.dot(expos[s], v_buf[s, 0], preferred_element_type=jnp.float32)
        outs.append(out / total)
    tail = tail_of(jnp.sum(logs, axis=0, keepdims=True))
    block = jnp.concatenate(outs + [tail], axis=0).astype(jnp.bfloat16)
    for d in range(8):
        packed[d] = block


def attention(query, keys, values, lengths, gain):
    f32, bf16 = jnp.float32, jnp.bfloat16
    whole = pl.BlockSpec(memory_space=pltpu.VMEM)
    return pl.pallas_call(
        attend,
        out_shape=(
            pltpu.VMEM((8, 72, 128), bf16),
            pltpu.VMEM((8, 128), f32),
        ),
        in_specs=[pl.BlockSpec(memory_space=pl.ANY)] * 5,
        out_specs=(whole,) * 2,
        scratch_shapes=[
            pltpu.VMEM(query.shape, bf16),
            pltpu.VMEM(keys.shape, bf16),
            pltpu.VMEM(values.shape, bf16),
            pltpu.SMEM(lengths.shape, jnp.int32),
            pltpu.VMEM((1, 128), bf16),
            pltpu.SemaphoreType.DMA((5,)),
        ],
        compiler_params=pltpu.CompilerParams(vmem_limit_bytes=60 * 2**20),
        name="attention",
    )(query, keys, values, lengths, gain.reshape(1, 128))


def near(blocks):
    return lax.all_to_all(blocks, KV, 0, 0, axis_index_groups=NEAR)


def far(blocks):
    return lax.all_to_all(blocks, "z", 0, 0, axis_index_groups=FAR)


def heads(blocks):
    return lax.all_to_all(blocks, HEAD, 0, 0)


def tail_of(logs):
    row = lax.broadcasted_iota(jnp.int32, (8, 128), 0)
    logs = jnp.broadcast_to(logs, (8, 128))
    high = logs.astype(jnp.bfloat16).astype(jnp.float32)
    middle = (logs - high).astype(jnp.bfloat16).astype(jnp.float32)
    low = logs - high - middle
    return jnp.where(row == 0, high, jnp.where(row == 1, middle, jnp.where(row == 2, low, 0.0)))


def merged(got):
    parts = [got[i].astype(jnp.float32) for i in range(8)]
    logs = jnp.concatenate([jnp.sum(p[64:72], axis=0, keepdims=True) for p in parts], axis=0)
    top = jnp.max(logs, axis=0, keepdims=True)
    share = jnp.exp(logs - top)
    total = jnp.sum(share, axis=0, keepdims=True)
    weights = jnp.transpose(share / total)
    outs = parts[0][0:64] * weights[0:64, 0:1]
    for i in range(1, 8):
        outs = outs + parts[i][0:64] * weights[0:64, i : i + 1]
    return outs, top + jnp.log(total)


def merge_near(got, packed):
    outs, logs = merged(got)
    block = jnp.concatenate([outs, tail_of(logs)], axis=0).astype(jnp.bfloat16)
    for i in range(8):
        packed[i] = block


def project(got, weight, terms, rows):
    rows[...] = merged(got)[0]
    attended = [rows[pl.ds(head, 8, stride=8), :] for head in range(8)]
    attended = jnp.concatenate(attended, axis=1).astype(jnp.bfloat16)
    product = jnp.dot(attended, weight[...], preferred_element_type=jnp.float32)
    for i in range(8):
        terms[i] = product


def summed(terms):
    total = terms[0].astype(jnp.float32)
    for i in range(1, 8):
        total = total + terms[i].astype(jnp.float32)
    return total, jnp.sum(total[7], axis=1, keepdims=True)


def row_tile(value):
    lane = lax.broadcasted_iota(jnp.int32, (8, 128), 1)
    value = jnp.broadcast_to(value, (8, 128))
    high = value.astype(jnp.bfloat16).astype(jnp.float32)
    middle = (value - high).astype(jnp.bfloat16).astype(jnp.float32)
    low = value - high - middle
    return jnp.where(lane == 0, high, jnp.where(lane == 1, middle, jnp.where(lane == 2, low, 0.0)))


def gate_up(terms, residual, gain, gate_weight, up_weight, hidden_out, packed):
    hidden = residual[...].astype(jnp.float32)
    projected = terms[0]
    for i in range(1, 8):
        projected = projected + terms[i]
    hidden = hidden + projected
    hidden_out[...] = hidden
    scaled = (hidden * gain[...]).astype(jnp.bfloat16)
    tile = row_tile(jnp.sum(hidden * hidden, axis=1, keepdims=True)).astype(jnp.bfloat16)
    for i in range(8):
        packed[i, 7] = tile
    for first, weight in ((0, gate_weight), (28, up_weight)):
        product = jnp.dot(scaled, weight[...], preferred_element_type=jnp.float32)
        for t in range(28):
            place = first + t
            packed[place // 7, place % 7] = product[:, 128 * t : 128 * t + 128].astype(jnp.bfloat16)


def sum_near(terms, packed):
    total, squares = summed(terms)
    block = jnp.concatenate([total[0:7], row_tile(squares)[None]], axis=0).astype(jnp.bfloat16)
    for i in range(8):
        packed[i] = block


def sum_far(terms, packed):
    total, squares = summed(terms)
    block = (total[0:7] * lax.rsqrt(squares / 8192 + 1e-05)[None]).astype(jnp.bfloat16)
    for i in range(8):
        packed[i] = block


def feed_down(got, weight, terms):
    tiles = []
    for t in range(28):
        gate = got[t // 7, t % 7].astype(jnp.float32)
        up = got[4 + t // 7, t % 7].astype(jnp.float32)
        tiles.append((gate / (1.0 + jnp.exp(-gate)) * up).astype(jnp.bfloat16))
    activated = jnp.concatenate(tiles, axis=1)
    product = jnp.dot(activated, weight[...], preferred_element_type=jnp.float32)
    for i in range(8):
        terms[i] = product


def step(body, shapes, count=1, scratch=()):
    whole = pl.BlockSpec(memory_space=pltpu.VMEM)
    return pl.pallas_call(
        body,
        out_shape=tuple(pltpu.VMEM(shape, dtype) for shape, dtype in shapes),
        in_specs=[whole] * count,
        out_specs=(whole,) * len(shapes),
        scratch_shapes=scratch,
        compiler_params=pltpu.CompilerParams(vmem_limit_bytes=4 * 2**20),
        name=body.__name__,
    )


def local(
    query,
    key_cache,
    value_cache,
    lengths,
    residual,
    out_weight,
    norm_gain,
    gate_weight,
    up_weight,
    down_weight,
):
    f32, bf16 = jnp.float32, jnp.bfloat16
    packed, gain = attention(query, key_cache, value_cache, lengths, norm_gain)
    (packed,) = step(merge_near, [((8, 72, 128), bf16)])(near(packed))
    rows = pltpu.VMEM((64, 128), f32)
    (terms,) = step(project, [((8, 8, 128), f32)], 2, [rows])(far(packed), out_weight)
    hidden_state, packed = step(gate_up, [((8, 128), f32), ((8, 8, 8, 128), bf16)], 5)(
        heads(terms), residual, gain, gate_weight, up_weight
    )
    (packed,) = step(sum_near, [((8, 8, 8, 128), bf16)])(near(packed))
    (packed,) = step(sum_far, [((8, 7, 8, 128), bf16)])(far(packed))
    (terms,) = step(feed_down, [((8, 8, 128), f32)], 2)(near(packed), down_weight)
    downward = jnp.sum(heads(terms), axis=0)
    return (hidden_state + downward).astype(bf16)


def solution(mesh):
    fine = Mesh(mesh.devices.reshape(SIZES), KV + HEAD)
    return jax.shard_map(
        local,
        mesh=fine,
        in_specs=(
            P(None, HEAD, None),
            P(None, HEAD, KV, None),
            P(None, HEAD, KV, None),
            P(),
            P(None, KV),
            P(HEAD, KV),
            P(KV),
            P(KV, HEAD),
            P(KV, HEAD),
            P(HEAD, KV),
        ),
        out_specs=P(None, KV),
        check_vma=False,
    )
```

```python
import math

import jax
import jax.numpy as jnp
from jax import lax
from jax.experimental import pallas as pl
from jax.experimental.pallas import tpu as pltpu
from jax.sharding import Mesh
from jax.sharding import PartitionSpec as P

KV = ("z", "x")
HEAD = ("y", "core")
SIZES = (16, 4, 4, 2)
FAR = [[2 * k + (k // 4 + half) % 2 for k in (4, 0, 5, 3, 6, 2, 7, 1)] for half in range(2)]
NEAR = [[FAR[half][k] * 4 + x for half in (1, 0) for x in (2, 0, 1, 3)] for k in range(8)]
HEADS = [[5, 7, 3, 1, 4, 6, 2, 0]]
NEG = -1e30


def attend(
    query, keys, values, lengths, gain, packed, gain_out,
    q_buf, k_buf, v_buf, l_buf, g_buf, s_sem,
):
    rows, _, block_len, _ = k_buf.shape
    small = [
        pltpu.make_async_copy(lengths, l_buf, s_sem.at[0]),
        pltpu.make_async_copy(query, q_buf, s_sem.at[1]),
        pltpu.make_async_copy(gain, g_buf, s_sem.at[2]),
    ]
    k_in = pltpu.make_async_copy(keys, k_buf, s_sem.at[3])
    v_in = pltpu.make_async_copy(values, v_buf, s_sem.at[4])
    for copy in small[0:2] + [k_in, v_in, small[2]]:
        copy.start()
    wide = (8, 128)
    row, lane = lax.broadcasted_iota(jnp.int32, wide, 0), lax.broadcasted_iota(jnp.int32, wide, 1)
    first = lax.axis_index(KV) * block_len
    place = first + lax.broadcasted_iota(jnp.int32, (8, block_len), 1)
    for copy in small:
        copy.wait()
    gain_out[...] = jnp.broadcast_to(g_buf[...].astype(jnp.float32), (8, 128))
    scores, live = [], []
    k_in.wait()
    for s in range(rows):
        product = lax.dot_general(
            q_buf[s], k_buf[s, 0], (((1,), (1,)), ((), ())), preferred_element_type=jnp.float32
        )
        scores.append(product * (1.0 / math.sqrt(128)))
        live.append(place < l_buf[s])
    tops, totals, expos = [], [], []
    for s in range(rows):
        masked = jnp.where(live[s], scores[s], NEG)
        top = jnp.max(masked, axis=1, keepdims=True)
        expo = jnp.where(live[s], jnp.exp(masked - top), 0.0)
        tops.append(top)
        totals.append(jnp.sum(expo, axis=1, keepdims=True))
        expos.append(expo.astype(jnp.bfloat16))
    outs, logs = [], jnp.zeros((8, 128), jnp.float32)
    v_in.wait()
    for s in range(rows):
        some = totals[s] > 0
        total = jnp.where(some, totals[s], 1.0)
        log = jnp.where(some, tops[s] + jnp.log(total), NEG)
        logs = logs + jnp.where(lane == row + 8 * s, jnp.broadcast_to(log, (8, 128)), 0.0)
        out = jnp.dot(expos[s], v_buf[s, 0], preferred_element_type=jnp.float32)
        outs.append(out / total)
    tail = tail_of(jnp.sum(logs, axis=0, keepdims=True))
    block = jnp.concatenate(outs + [tail], axis=0).astype(jnp.bfloat16)
    for d in range(8):
        packed[d] = block


def attention(query, keys, values, lengths, gain):
    f32, bf16 = jnp.float32, jnp.bfloat16
    whole = pl.BlockSpec(memory_space=pltpu.VMEM)
    return pl.pallas_call(
        attend,
        out_shape=(
            pltpu.VMEM((8, 72, 128), bf16),
            pltpu.VMEM((8, 128), f32),
        ),
        in_specs=[pl.BlockSpec(memory_space=pl.ANY)] * 5,
        out_specs=(whole,) * 2,
        scratch_shapes=[
            pltpu.VMEM(query.shape, bf16),
            pltpu.VMEM(keys.shape, bf16),
            pltpu.VMEM(values.shape, bf16),
            pltpu.SMEM(lengths.shape, jnp.int32),
            pltpu.VMEM((1, 128), bf16),
            pltpu.SemaphoreType.DMA((5,)),
        ],
        compiler_params=pltpu.CompilerParams(vmem_limit_bytes=60 * 2**20),
        name="attention",
    )(query, keys, values, lengths, gain.reshape(1, 128))


def near(blocks):
    return lax.all_to_all(blocks, KV, 0, 0, axis_index_groups=NEAR)


def far(blocks):
    return lax.all_to_all(blocks, "z", 0, 0, axis_index_groups=FAR)


def heads(blocks):
    return lax.all_to_all(blocks, HEAD, 0, 0, axis_index_groups=HEADS)


def tail_of(logs):
    row = lax.broadcasted_iota(jnp.int32, (8, 128), 0)
    logs = jnp.broadcast_to(logs, (8, 128))
    high = logs.astype(jnp.bfloat16).astype(jnp.float32)
    middle = (logs - high).astype(jnp.bfloat16).astype(jnp.float32)
    low = logs - high - middle
    return jnp.where(row == 0, high, jnp.where(row == 1, middle, jnp.where(row == 2, low, 0.0)))


def merged(got):
    parts = [got[i].astype(jnp.float32) for i in range(8)]
    logs = jnp.concatenate([jnp.sum(p[64:72], axis=0, keepdims=True) for p in parts], axis=0)
    top = jnp.max(logs, axis=0, keepdims=True)
    share = jnp.exp(logs - top)
    total = jnp.sum(share, axis=0, keepdims=True)
    weights = jnp.transpose(share / total)
    outs = parts[0][0:64] * weights[0:64, 0:1]
    for i in range(1, 8):
        outs = outs + parts[i][0:64] * weights[0:64, i : i + 1]
    return outs, top + jnp.log(total)


def merge_near(got, packed):
    outs, logs = merged(got)
    block = jnp.concatenate([outs, tail_of(logs)], axis=0).astype(jnp.bfloat16)
    for i in range(8):
        packed[i] = block


def project(got, weight, terms, rows):
    rows[...] = merged(got)[0]
    attended = [rows[pl.ds(head, 8, stride=8), :] for head in range(8)]
    attended = jnp.concatenate(attended, axis=1).astype(jnp.bfloat16)
    product = jnp.dot(attended, weight[...], preferred_element_type=jnp.float32)
    for i in range(8):
        terms[i] = product


def summed(terms):
    total = terms[0].astype(jnp.float32)
    for i in range(1, 8):
        total = total + terms[i].astype(jnp.float32)
    return total, jnp.sum(total[7], axis=1, keepdims=True)


def row_tile(value):
    lane = lax.broadcasted_iota(jnp.int32, (8, 128), 1)
    value = jnp.broadcast_to(value, (8, 128))
    high = value.astype(jnp.bfloat16).astype(jnp.float32)
    middle = (value - high).astype(jnp.bfloat16).astype(jnp.float32)
    low = value - high - middle
    return jnp.where(lane == 0, high, jnp.where(lane == 1, middle, jnp.where(lane == 2, low, 0.0)))


def gate_up(terms, residual, gain, gate_weight, up_weight, hidden_out, packed):
    hidden = residual[...].astype(jnp.float32)
    projected = terms[0]
    for i in range(1, 8):
        projected = projected + terms[i]
    hidden = hidden + projected
    hidden_out[...] = hidden
    scaled = (hidden * gain[...]).astype(jnp.bfloat16)
    tile = row_tile(jnp.sum(hidden * hidden, axis=1, keepdims=True)).astype(jnp.bfloat16)
    for i in range(8):
        packed[i, 7] = tile
    for first, weight in ((0, gate_weight), (28, up_weight)):
        product = jnp.dot(scaled, weight[...], preferred_element_type=jnp.float32)
        for t in range(28):
            place = first + t
            packed[place // 7, place % 7] = product[:, 128 * t : 128 * t + 128].astype(jnp.bfloat16)


def sum_near(terms, packed):
    total, squares = summed(terms)
    block = jnp.concatenate([total[0:7], row_tile(squares)[None]], axis=0).astype(jnp.bfloat16)
    for i in range(8):
        packed[i] = block


def sum_far(terms, packed):
    total, squares = summed(terms)
    block = (total[0:7] * lax.rsqrt(squares / 8192 + 1e-05)[None]).astype(jnp.bfloat16)
    for i in range(8):
        packed[i] = block


def feed_down(got, weight, terms):
    tiles = []
    for t in range(28):
        gate = got[t // 7, t % 7].astype(jnp.float32)
        up = got[4 + t // 7, t % 7].astype(jnp.float32)
        tiles.append((gate / (1.0 + jnp.exp(-gate)) * up).astype(jnp.bfloat16))
    activated = jnp.concatenate(tiles, axis=1)
    product = jnp.dot(activated, weight[...], preferred_element_type=jnp.float32)
    for i in range(8):
        terms[i] = product


def step(body, shapes, count=1, scratch=()):
    whole = pl.BlockSpec(memory_space=pltpu.VMEM)
    return pl.pallas_call(
        body,
        out_shape=tuple(pltpu.VMEM(shape, dtype) for shape, dtype in shapes),
        in_specs=[whole] * count,
        out_specs=(whole,) * len(shapes),
        scratch_shapes=scratch,
        compiler_params=pltpu.CompilerParams(vmem_limit_bytes=4 * 2**20),
        name=body.__name__,
    )


def local(
    query,
    key_cache,
    value_cache,
    lengths,
    residual,
    out_weight,
    norm_gain,
    gate_weight,
    up_weight,
    down_weight,
):
    f32, bf16 = jnp.float32, jnp.bfloat16
    packed, gain = attention(query, key_cache, value_cache, lengths, norm_gain)
    (packed,) = step(merge_near, [((8, 72, 128), bf16)])(near(packed))
    rows = pltpu.VMEM((64, 128), f32)
    (terms,) = step(project, [((8, 8, 128), f32)], 2, [rows])(far(packed), out_weight)
    hidden_state, packed = step(gate_up, [((8, 128), f32), ((8, 8, 8, 128), bf16)], 5)(
        heads(terms), residual, gain, gate_weight, up_weight
    )
    (packed,) = step(sum_near, [((8, 8, 8, 128), bf16)])(near(packed))
    (packed,) = step(sum_far, [((8, 7, 8, 128), bf16)])(far(packed))
    (terms,) = step(feed_down, [((8, 8, 128), f32)], 2)(near(packed), down_weight)
    downward = jnp.sum(heads(terms), axis=0)
    return (hidden_state + downward).astype(bf16)


def solution(mesh):
    fine = Mesh(mesh.devices.reshape(SIZES), KV + HEAD)
    return jax.shard_map(
        local,
        mesh=fine,
        in_specs=(
            P(None, HEAD, None),
            P(None, HEAD, KV, None),
            P(None, HEAD, KV, None),
            P(),
            P(None, KV),
            P(HEAD, KV),
            P(KV),
            P(KV, HEAD),
            P(KV, HEAD),
            P(HEAD, KV),
        ),
        out_specs=P(None, KV),
        check_vma=False,
    )
```

```python
import math

import jax
import jax.numpy as jnp
from jax import lax
from jax.experimental import pallas as pl
from jax.experimental.pallas import tpu as pltpu
from jax.sharding import Mesh
from jax.sharding import PartitionSpec as P

KV = ("z", "x")
HEAD = ("y", "core")
SIZES = (16, 4, 4, 2)
FAR = [[2 * k + (k // 4 + half) % 2 for k in (4, 0, 5, 3, 6, 2, 7, 1)] for half in range(2)]
NEAR = [[FAR[half][k] * 4 + x for half in (0, 1) for x in (2, 0, 1, 3)] for k in range(8)]
HEADS = [[5, 7, 3, 1, 4, 6, 2, 0]]
NEG = -1e30


def attend(
    query, keys, values, lengths, gain, packed, gain_out,
    q_buf, k_buf, v_buf, l_buf, g_buf, s_sem,
):
    rows, _, block_len, _ = k_buf.shape
    small = [
        pltpu.make_async_copy(lengths, l_buf, s_sem.at[0]),
        pltpu.make_async_copy(query, q_buf, s_sem.at[1]),
        pltpu.make_async_copy(gain, g_buf, s_sem.at[2]),
    ]
    k_in = pltpu.make_async_copy(keys, k_buf, s_sem.at[3])
    v_in = pltpu.make_async_copy(values, v_buf, s_sem.at[4])
    for copy in small[0:2] + [k_in, v_in, small[2]]:
        copy.start()
    wide = (8, 128)
    row, lane = lax.broadcasted_iota(jnp.int32, wide, 0), lax.broadcasted_iota(jnp.int32, wide, 1)
    first = lax.axis_index(KV) * block_len
    place = first + lax.broadcasted_iota(jnp.int32, (8, block_len), 1)
    for copy in small:
        copy.wait()
    gain_out[...] = jnp.broadcast_to(g_buf[...].astype(jnp.float32), (8, 128))
    scores, live = [], []
    k_in.wait()
    for s in range(rows):
        product = lax.dot_general(
            q_buf[s], k_buf[s, 0], (((1,), (1,)), ((), ())), preferred_element_type=jnp.float32
        )
        scores.append(product * (1.0 / math.sqrt(128)))
        live.append(place < l_buf[s])
    tops, totals, expos = [], [], []
    for s in range(rows):
        masked = jnp.where(live[s], scores[s], NEG)
        top = jnp.max(masked, axis=1, keepdims=True)
        expo = jnp.where(live[s], jnp.exp(masked - top), 0.0)
        tops.append(top)
        totals.append(jnp.sum(expo, axis=1, keepdims=True))
        expos.append(expo.astype(jnp.bfloat16))
    outs, logs = [], jnp.zeros((8, 128), jnp.float32)
    v_in.wait()
    for s in range(rows):
        some = totals[s] > 0
        total = jnp.where(some, totals[s], 1.0)
        log = jnp.where(some, tops[s] + jnp.log(total), NEG)
        logs = logs + jnp.where(lane == row + 8 * s, jnp.broadcast_to(log, (8, 128)), 0.0)
        out = jnp.dot(expos[s], v_buf[s, 0], preferred_element_type=jnp.float32)
        outs.append(out / total)
    tail = tail_of(jnp.sum(logs, axis=0, keepdims=True))
    block = jnp.concatenate(outs + [tail], axis=0).astype(jnp.bfloat16)
    for d in range(8):
        packed[d] = block


def attention(query, keys, values, lengths, gain):
    f32, bf16 = jnp.float32, jnp.bfloat16
    whole = pl.BlockSpec(memory_space=pltpu.VMEM)
    return pl.pallas_call(
        attend,
        out_shape=(
            pltpu.VMEM((8, 72, 128), bf16),
            pltpu.VMEM((8, 128), f32),
        ),
        in_specs=[pl.BlockSpec(memory_space=pl.ANY)] * 5,
        out_specs=(whole,) * 2,
        scratch_shapes=[
            pltpu.VMEM(query.shape, bf16),
            pltpu.VMEM(keys.shape, bf16),
            pltpu.VMEM(values.shape, bf16),
            pltpu.SMEM(lengths.shape, jnp.int32),
            pltpu.VMEM((1, 128), bf16),
            pltpu.SemaphoreType.DMA((5,)),
        ],
        compiler_params=pltpu.CompilerParams(vmem_limit_bytes=60 * 2**20),
        name="attention",
    )(query, keys, values, lengths, gain.reshape(1, 128))


def near(blocks):
    return lax.all_to_all(blocks, KV, 0, 0, axis_index_groups=NEAR)


def far(blocks):
    return lax.all_to_all(blocks, "z", 0, 0, axis_index_groups=FAR)


def heads(blocks):
    return lax.all_to_all(blocks, HEAD, 0, 0, axis_index_groups=HEADS)


def tail_of(logs):
    row = lax.broadcasted_iota(jnp.int32, (8, 128), 0)
    logs = jnp.broadcast_to(logs, (8, 128))
    high = logs.astype(jnp.bfloat16).astype(jnp.float32)
    middle = (logs - high).astype(jnp.bfloat16).astype(jnp.float32)
    low = logs - high - middle
    return jnp.where(row == 0, high, jnp.where(row == 1, middle, jnp.where(row == 2, low, 0.0)))


def merged(got):
    parts = [got[i].astype(jnp.float32) for i in range(8)]
    logs = jnp.concatenate([jnp.sum(p[64:72], axis=0, keepdims=True) for p in parts], axis=0)
    top = jnp.max(logs, axis=0, keepdims=True)
    share = jnp.exp(logs - top)
    total = jnp.sum(share, axis=0, keepdims=True)
    weights = jnp.transpose(share / total)
    outs = parts[0][0:64] * weights[0:64, 0:1]
    for i in range(1, 8):
        outs = outs + parts[i][0:64] * weights[0:64, i : i + 1]
    return outs, top + jnp.log(total)


def merge_near(got, packed):
    outs, logs = merged(got)
    block = jnp.concatenate([outs, tail_of(logs)], axis=0).astype(jnp.bfloat16)
    for i in range(8):
        packed[i] = block


def project(got, weight, terms, rows):
    rows[...] = merged(got)[0]
    attended = [rows[pl.ds(head, 8, stride=8), :] for head in range(8)]
    attended = jnp.concatenate(attended, axis=1).astype(jnp.bfloat16)
    product = jnp.dot(attended, weight[...], preferred_element_type=jnp.float32)
    for i in range(8):
        terms[i] = product


def summed(terms):
    total = terms[0].astype(jnp.float32)
    for i in range(1, 8):
        total = total + terms[i].astype(jnp.float32)
    return total, jnp.sum(total[7], axis=1, keepdims=True)


def row_tile(value):
    lane = lax.broadcasted_iota(jnp.int32, (8, 128), 1)
    value = jnp.broadcast_to(value, (8, 128))
    high = value.astype(jnp.bfloat16).astype(jnp.float32)
    middle = (value - high).astype(jnp.bfloat16).astype(jnp.float32)
    low = value - high - middle
    return jnp.where(lane == 0, high, jnp.where(lane == 1, middle, jnp.where(lane == 2, low, 0.0)))


def gate_up(terms, residual, gain, gate_weight, up_weight, hidden_out, packed):
    hidden = residual[...].astype(jnp.float32)
    projected = terms[0]
    for i in range(1, 8):
        projected = projected + terms[i]
    hidden = hidden + projected
    hidden_out[...] = hidden
    scaled = (hidden * gain[...]).astype(jnp.bfloat16)
    tile = row_tile(jnp.sum(hidden * hidden, axis=1, keepdims=True)).astype(jnp.bfloat16)
    for i in range(8):
        packed[i, 7] = tile
    for first, weight in ((0, gate_weight), (28, up_weight)):
        product = jnp.dot(scaled, weight[...], preferred_element_type=jnp.float32)
        for t in range(28):
            place = first + t
            packed[place // 7, place % 7] = product[:, 128 * t : 128 * t + 128].astype(jnp.bfloat16)


def sum_near(terms, packed):
    total, squares = summed(terms)
    block = jnp.concatenate([total[0:7], row_tile(squares)[None]], axis=0).astype(jnp.bfloat16)
    for i in range(8):
        packed[i] = block


def sum_far(terms, packed):
    total, squares = summed(terms)
    block = (total[0:7] * lax.rsqrt(squares / 8192 + 1e-05)[None]).astype(jnp.bfloat16)
    for i in range(8):
        packed[i] = block


def feed_down(got, weight, terms):
    tiles = []
    for t in range(28):
        gate = got[t // 7, t % 7].astype(jnp.float32)
        up = got[4 + t // 7, t % 7].astype(jnp.float32)
        tiles.append((gate / (1.0 + jnp.exp(-gate)) * up).astype(jnp.bfloat16))
    activated = jnp.concatenate(tiles, axis=1)
    product = jnp.dot(activated, weight[...], preferred_element_type=jnp.float32)
    for i in range(8):
        terms[i] = product


def step(body, shapes, count=1, scratch=()):
    whole = pl.BlockSpec(memory_space=pltpu.VMEM)
    return pl.pallas_call(
        body,
        out_shape=tuple(pltpu.VMEM(shape, dtype) for shape, dtype in shapes),
        in_specs=[whole] * count,
        out_specs=(whole,) * len(shapes),
        scratch_shapes=scratch,
        compiler_params=pltpu.CompilerParams(vmem_limit_bytes=4 * 2**20),
        name=body.__name__,
    )


def local(
    query,
    key_cache,
    value_cache,
    lengths,
    residual,
    out_weight,
    norm_gain,
    gate_weight,
    up_weight,
    down_weight,
):
    f32, bf16 = jnp.float32, jnp.bfloat16
    packed, gain = attention(query, key_cache, value_cache, lengths, norm_gain)
    (packed,) = step(merge_near, [((8, 72, 128), bf16)])(near(packed))
    rows = pltpu.VMEM((64, 128), f32)
    (terms,) = step(project, [((8, 8, 128), f32)], 2, [rows])(far(packed), out_weight)
    hidden_state, packed = step(gate_up, [((8, 128), f32), ((8, 8, 8, 128), bf16)], 5)(
        heads(terms), residual, gain, gate_weight, up_weight
    )
    (packed,) = step(sum_near, [((8, 8, 8, 128), bf16)])(near(packed))
    (packed,) = step(sum_far, [((8, 7, 8, 128), bf16)])(far(packed))
    (terms,) = step(feed_down, [((8, 8, 128), f32)], 2)(near(packed), down_weight)
    downward = jnp.sum(heads(terms), axis=0)
    return (hidden_state + downward).astype(bf16)


def solution(mesh):
    fine = Mesh(mesh.devices.reshape(SIZES), KV + HEAD)
    return jax.shard_map(
        local,
        mesh=fine,
        in_specs=(
            P(None, HEAD, None),
            P(None, HEAD, KV, None),
            P(None, HEAD, KV, None),
            P(),
            P(None, KV),
            P(HEAD, KV),
            P(KV),
            P(KV, HEAD),
            P(KV, HEAD),
            P(HEAD, KV),
        ),
        out_specs=P(None, KV),
        check_vma=False,
    )
```
